32 devices in a mesh: tm: 2 (over x), height: 8 (over z, y), batch: 2 (over core).
Axes of the slice: x: 2, y: 2, z: 4, core: 2. Of those that a mesh axis runs over, the one named last changes fastest.
Arguments:
- conv_input: bfloat16 [2, 4, 8, 64, 384], P('batch', 'tm', 'height'), may hold values from -6 to 6
- saved: bfloat16 [2, 4, 8, 64, 384], P('batch', 'tm', 'height'), may hold values from -6 to 6
- cotangent: bfloat16 [2, 4, 8, 64, 384], P('batch', 'tm', 'height'), may hold values from -6 to 6
- gain: float32 [384], replicated, may hold values from 0.1 to 1.9
- w_conv: bfloat16 [3, 3, 3, 384, 384], replicated, may hold values from -0.0625 to 0.0625
- w_qkv: bfloat16 [384, 1152], replicated, may hold values from -4 to 4
- w_out: bfloat16 [384, 384], replicated, may hold values from -0.3125 to 0.3125
Outputs:
- input_grad: bfloat16 [2, 4, 8, 64, 384], P('batch', 'tm', 'height')
- weight_grad: float32 [384, 27, 384], P('height')
The draws below stay inside these ranges and needn't reach their ends.
All inputs are finite; a program needn't handle non-finite values.
Results may differ from the reference program's by a relative error of at most 0.015.
Values may be sent and summed in bfloat16 or wider, within the bound.
A program may use at most 128 MiB of HBM per device.

```python
import math
import jax
import jax.numpy as jnp
from jax import lax

CH = 384
HB = 1
WCOL = 64
CLIPS = 2
FRAMES = 4
ROWS = 8
KEYS = 512
POSITIONS = 4096
N_HEIGHT = 8


def draw_w_qkv(key, part):
    key = jax.random.fold_in(key, 7)
    base_key = jax.random.fold_in(key, 0)
    matrix = jax.random.normal(base_key, (CH, 3 * CH), jnp.float32) / math.sqrt(CH)
    return matrix.astype(jnp.bfloat16)


def levels(stream_key, dims, cuts, low, largest):
    loudness = 1.0
    for dim, blocks in cuts:
        draws = jax.random.uniform(jax.random.fold_in(jax.random.fold_in(stream_key, 6), dim), (blocks,), jnp.float32, low / len(cuts), largest / len(cuts))
        loudness = loudness * jnp.repeat(jnp.exp(draws), dims[dim] // blocks).reshape((-1,) + (1,) * (len(dims) - 1 - dim))
    return loudness


def noise(rng, shape, deviation, most, cuts=(), kind=jnp.bfloat16):
    level = levels(rng, shape, cuts, -0.22, 0.18) if cuts else 1.0
    drawn = jax.random.normal(rng, shape, jnp.float32) * deviation * level
    return jnp.minimum(jnp.maximum(drawn, -most), most).astype(kind)


def setup_inputs(seed: int = 0) -> dict:
    splits = jax.random.split(jax.random.key(seed), 8)
    conv_input = noise(splits[0], (CLIPS, FRAMES, ROWS, WCOL, CH), 1.0, 6.0, ((0, 2), (1, 2), (2, 8)))
    saved = noise(splits[1], (CLIPS, FRAMES, ROWS, WCOL, CH), 1.0, 6.0, ((0, 2), (1, 2), (2, 8)))
    cotangent = noise(splits[2], (CLIPS, FRAMES, ROWS, WCOL, CH), 1.0, 6.0, ((0, 2), (1, 2), (2, 8)))
    gain = jnp.clip(1.0 + 0.18 * jax.random.normal(splits[3], (CH,), jnp.float32), 0.1, 1.9)
    w_conv = noise(splits[4], (3, 3, 3, CH, CH), (27 * CH) ** -0.5, 0.0625)
    w_qkv = draw_w_qkv(jax.random.fold_in(splits[7], 71), 0)
    w_out = noise(splits[6], (CH, CH), CH ** -0.5, 0.3125)
    return dict(conv_input=conv_input, saved=saved, cotangent=cotangent, gain=gain, w_conv=w_conv, w_qkv=w_qkv, w_out=w_out)


EPS = 1e-06

def reference(conv_input, saved, cotangent, gain, w_conv, w_qkv, w_out):
    scale = 1.0 / math.sqrt(CH)
    band = HB * WCOL
    hidden = saved.astype(jnp.float32)
    inverse = lax.rsqrt(lax.optimization_barrier(jnp.mean(hidden * hidden, -1, keepdims=True)) + EPS)
    normed = (hidden * inverse * gain).astype(jnp.bfloat16)
    qkv = jnp.dot(normed.reshape(-1, CH), w_qkv, preferred_element_type=jnp.float32).astype(jnp.bfloat16)
    qkv = qkv.reshape(CLIPS * FRAMES, KEYS, 3 * CH)
    grad_out = jnp.dot(cotangent.reshape(-1, CH), w_out.T, preferred_element_type=jnp.float32).astype(jnp.bfloat16)
    grad_out = grad_out.reshape(CLIPS * FRAMES, KEYS, CH)

    def attend_frame(pair):
        frame_qkv, frame_grad = pair
        queries = frame_qkv[:, :CH]
        keys = frame_qkv[:, CH:2 * CH]
        values = frame_qkv[:, 2 * CH:]
        scores = jnp.dot(queries, keys.T, preferred_element_type=jnp.float32) * scale
        probs = jax.nn.softmax(scores, axis=-1)
        probs_low = probs.astype(jnp.bfloat16)
        grad_probs = jnp.dot(frame_grad, values.T, preferred_element_type=jnp.float32)
        delta = lax.optimization_barrier(jnp.sum(probs * grad_probs, -1, keepdims=True))
        grad_scores = (probs * (grad_probs - delta) * scale).astype(jnp.bfloat16)
        grad_q = jnp.dot(grad_scores, keys, preferred_element_type=jnp.float32).astype(jnp.bfloat16)
        key_parts = jnp.einsum('gqk,gqc->gkc', grad_scores.reshape(N_HEIGHT, band, KEYS).astype(jnp.float32), queries.reshape(N_HEIGHT, band, CH).astype(jnp.float32)).astype(jnp.bfloat16)
        value_parts = jnp.einsum('gqk,gqc->gkc', probs_low.reshape(N_HEIGHT, band, KEYS).astype(jnp.float32), frame_grad.reshape(N_HEIGHT, band, CH).astype(jnp.float32)).astype(jnp.bfloat16)
        grad_k = lax.optimization_barrier(jnp.sum(key_parts.astype(jnp.float32), 0)).astype(jnp.bfloat16)
        grad_v = lax.optimization_barrier(jnp.sum(value_parts.astype(jnp.float32), 0)).astype(jnp.bfloat16)
        return jnp.concatenate([grad_q, grad_k, grad_v], -1)
    grad_qkv = lax.map(attend_frame, (qkv, grad_out))
    grad_normed = jnp.dot(grad_qkv.reshape(-1, 3 * CH), w_qkv.T, preferred_element_type=jnp.float32)
    scaled = grad_normed.reshape(hidden.shape) * gain
    grad_saved = (cotangent.astype(jnp.float32) + inverse * (scaled - hidden * inverse * inverse * lax.optimization_barrier(jnp.mean(scaled * hidden, -1, keepdims=True)))).astype(jnp.bfloat16)
    padded = jnp.pad(grad_saved, ((0, 0), (0, 2), (1, 1), (1, 1), (0, 0)))
    inputs_flat = conv_input.reshape(-1, CH)
    grad_input = jnp.zeros((CLIPS * FRAMES * ROWS * WCOL, CH), jnp.float32)
    kernel_taps = []
    for tap_t in range(3):
        for tap_r in range(3):
            for tap_c in range(3):
                window = padded[:, 2 - tap_t:2 - tap_t + FRAMES, 2 - tap_r:2 - tap_r + ROWS, 2 - tap_c:2 - tap_c + WCOL].reshape(-1, CH)
                grad_input = grad_input + jnp.dot(window, w_conv[tap_t, tap_r, tap_c].T, preferred_element_type=jnp.float32)
                kernel_taps.append(jnp.dot(inputs_flat.T, window, preferred_element_type=jnp.float32))
    weight_grad = jnp.stack(kernel_taps, 1) / math.sqrt(POSITIONS)
    return (grad_input.reshape(conv_input.shape).astype(jnp.bfloat16), weight_grad)
```

```python
import functools
import math

import jax
import jax.numpy as jnp
from jax import lax
from jax.experimental import pallas as pl
from jax.experimental.pallas import tpu as pltpu
from jax.sharding import PartitionSpec as P

EPS = 1e-06
NT = (((1,), (1,)), ((), ()))
TN = (((0,), (0,)), ((), ()))
F32 = jnp.float32
BF16 = jnp.bfloat16


def mm(x, y):
    return jnp.dot(x, y, preferred_element_type=F32)


def mm_nt(x, y):
    return lax.dot_general(x, y, NT, preferred_element_type=F32)


def mm_tn(x, y):
    return lax.dot_general(x, y, TN, preferred_element_type=F32)


def body(
    sizes,
    saved_ref, cot_ref, conv_ref, gain_ref, wqkv_hbm, wout_hbm, wconv_hbm,
    igrad_ref, wgrad_ref,
    wqkv, wout, wconv, xall, conv_t, recv_t, gpad, lhs, win,
    part_f, part_b, half_f, half_b, got1, got2, total, ig_send, ig_got,
    wsem, gs_sem, gr_sem, cs_sem, cr_sem, is_sem, ir_sem,
    s1s, s1r, s2s, s2r, s3s, s3r, s4s, s4r,
):
    n_t, n_h, n_b, frames, columns, chans, tp = sizes
    tile = frames * columns
    dblk = chans // n_h
    n_a = n_h // 2
    ht = n_t * tp
    t = lax.axis_index("tm")
    h = lax.axis_index("height")
    c = lax.axis_index("batch")
    scale = 1.0 / math.sqrt(chans)
    norm = 1.0 / math.sqrt(n_b * n_t * frames * n_h * columns)

    loads = [
        pltpu.make_async_copy(wqkv_hbm, wqkv, wsem.at[0]),
        pltpu.make_async_copy(wout_hbm, wout, wsem.at[1]),
        pltpu.make_async_copy(wconv_hbm, wconv, wsem.at[2]),
    ]
    for load in loads:
        load.start()

    def remote(src, dst, ssem, rsem, dev):
        return pltpu.make_async_remote_copy(
            src_ref=src, dst_ref=dst, send_sem=ssem, recv_sem=rsem,
            device_id=dev, device_id_type=pl.DeviceIdType.MESH,
        )

    barrier = pltpu.get_barrier_semaphore()
    for dt in range(n_t):
        for dh in range(n_h):
            if dt or dh:
                pl.semaphore_signal(
                    barrier, inc=1,
                    device_id=(lax.rem(t + dt, n_t), lax.rem(h + dh, n_h), c),
                    device_id_type=pl.DeviceIdType.MESH,
                )
    for db in range(1, n_b):
        pl.semaphore_signal(
            barrier, inc=1, device_id=(t, h, lax.rem(c + db, n_b)),
            device_id_type=pl.DeviceIdType.MESH,
        )
    pl.semaphore_wait(barrier, n_t * n_h - 1 + n_b - 1)

    h_a, h_b = h // 2, lax.rem(h, 2)
    mate = h_a * 2 + (1 - h_b)
    order = sorted(range(1, n_a), key=lambda k: min(k, n_a - k))
    sends = []
    mine = (saved_ref, cot_ref)
    for arr in range(2):
        for k in order:
            peer = lax.rem(h_a + k, n_a) * 2 + h_b
            cp = remote(mine[arr], xall.at[arr, h], gs_sem.at[arr, k], gr_sem.at[arr, h], (t, peer, c))
            cp.start()
            sends.append(cp)
        cp = remote(mine[arr], xall.at[arr, h], gs_sem.at[arr, 0], gr_sem.at[arr, h], (t, mate, c))
        cp.start()
        sends.append(cp)
    for arr in range(2):
        xall[arr, h] = mine[arr][...]

    flipped = conv_ref[...].astype(F32).T.astype(BF16)
    for k in range(n_h):
        conv_t[k] = flipped[k * dblk:(k + 1) * dblk]
    recv_t[0, h] = conv_t[h]

    for arr in range(2):
        for k in order:
            src = lax.rem(h_a + k, n_a) * 2 + h_b
            remote(mine[arr], xall.at[arr, src], gs_sem.at[arr, k], gr_sem.at[arr, src], (t, mate, c)).wait_recv()
            cp = remote(xall.at[arr, src], xall.at[arr, src], gs_sem.at[arr, n_a + k - 1], gr_sem.at[arr, src], (t, mate, c))
            cp.start()
            sends.append(cp)

    for k in range(1, n_h):
        peer = lax.rem(h + k, n_h)
        cp = remote(conv_t.at[peer], recv_t.at[0, h], cs_sem.at[0, k], cr_sem.at[0, h], (t, peer, c))
        cp.start()
        sends.append(cp)

    def to_next(k):
        peer = lax.rem(h + k, n_h)
        later = jnp.minimum(t + 1, n_t - 1)
        return remote(conv_t.at[peer], recv_t.at[1, h], cs_sem.at[1, k], cr_sem.at[1, h], (later, peer, c))

    @pl.when(t < n_t - 1)
    def _():
        for k in range(n_h):
            to_next(k).start()

    @pl.when(t == 0)
    def _():
        recv_t[1] = jnp.zeros_like(recv_t[1])

    for arr in range(2):
        for k in range(n_a):
            src = lax.rem(h_a + k, n_a) * 2 + (1 - h_b)
            remote(mine[arr], xall.at[arr, src], gs_sem.at[arr, 0], gr_sem.at[arr, src], (t, mate, c)).wait_recv()

    loads[0].wait()
    loads[1].wait()
    gain = gain_ref[...]
    keys_n = n_h * columns
    gpad[0] = jnp.zeros_like(gpad[0])
    gpad[n_h + 1] = jnp.zeros_like(gpad[0])

    def frame(f, carry):
        rows = pl.ds(pl.multiple_of(f * columns, columns), columns)
        hidden = xall[0, :, rows, :].reshape(keys_n, chans).astype(F32)
        cot = xall[1, :, rows, :].reshape(keys_n, chans)
        inverse = lax.rsqrt(jnp.mean(hidden * hidden, -1, keepdims=True) + EPS)
        normed = (hidden * inverse * gain).astype(BF16)
        qkv = mm(normed, wqkv[...]).astype(BF16)
        q, k, v = qkv[:, :chans], qkv[:, chans:2 * chans], qkv[:, 2 * chans:]
        go = mm_nt(cot, wout[...]).astype(BF16)
        s = mm_nt(k, q) * scale
        e = jnp.exp(s - jnp.max(s, 0, keepdims=True))
        p = e / jnp.sum(e, 0, keepdims=True)
        gp = mm_nt(v, go)
        delta = jnp.sum(p * gp, 0, keepdims=True)
        gs = (p * (gp - delta) * scale).astype(BF16)
        gq = mm_tn(gs, k).astype(BF16)
        gk = mm(gs, q).astype(BF16)
        gv = mm(p.astype(BF16), go).astype(BF16)
        gn = (
            mm_nt(gq, wqkv[:, :chans])
            + mm_nt(gk, wqkv[:, chans:2 * chans])
            + mm_nt(gv, wqkv[:, 2 * chans:])
        )
        scaled = gn * gain
        g = cot.astype(F32) + inverse * (
            scaled - hidden * inverse * inverse * jnp.mean(scaled * hidden, -1, keepdims=True)
        )
        gpad[1:n_h + 1, rows, :] = g.astype(BF16).reshape(n_h, columns, chans)
        return carry

    lax.fori_loop(0, frames, frame, 0)

    for k in range(1, n_h):
        src = lax.rem(h + k, n_h)
        remote(conv_t.at[0], recv_t.at[0, src], cs_sem.at[0, k], cr_sem.at[0, src], (t, src, c)).wait_recv()

    @pl.when(t > 0)
    def _():
        for k in range(n_h):
            src = lax.rem(h + k, n_h)
            remote(conv_t.at[0], recv_t.at[1, src], cs_sem.at[1, k], cr_sem.at[1, src], (t, mate, c)).wait_recv()

    lane = lax.broadcasted_iota(jnp.int32, (dblk, tile), 1)
    for a in range(3):
        for j in range(3):
            lhs[3 * a + j, 0] = jnp.zeros((dblk, tile), BF16)
            lhs[3 * a + j, n_h + 1] = jnp.zeros((dblk, tile), BF16)

    def shifts(r, carry):
        own = recv_t[0, r].astype(F32)
        prev = recv_t[1, r].astype(F32)
        both = jnp.where(lane < columns, pltpu.roll(prev, columns, 1), pltpu.roll(own, columns, 1))
        for a, x in enumerate((prev, both, own)):
            left = jnp.where(lax.rem(lane, columns) == 0, 0.0, pltpu.roll(x, 1, 1))
            right = jnp.where(lax.rem(lane, columns) == columns - 1, 0.0, pltpu.roll(x, tile - 1, 1))
            for j, y in enumerate((left, x, right)):
                lhs[3 * a + j, r + 1] = y.astype(BF16)
        return carry

    lax.fori_loop(0, n_h, shifts, 0)

    for b in range(3):
        rights = gpad[1:n_h + 1].reshape(n_h * tile, chans)
        left = jnp.concatenate(
            [lhs[:, b + r].reshape(9 * dblk, tile) for r in range(n_h)], axis=1
        )
        out = (mm(left, rights) * norm).reshape(9, dblk, chans)
        for a in range(3):
            for j in range(3):
                tap = 9 * a + 3 * b + j
                part_f[tap] = out[3 * a + j]
                part_b[tap] = out[3 * a + j].astype(BF16)
    for tap in range(27, n_b * ht):
        part_f[tap] = jnp.zeros((dblk, chans), F32)
        part_b[tap] = jnp.zeros((dblk, chans), BF16)

    for k in range(1, n_b):
        peer = lax.rem(c + k, n_b)
        cp = remote(part_b.at[pl.ds(peer * ht, ht)], got1.at[c], s1s.at[k], s1r.at[c], (t, h, peer))
        cp.start()
        sends.append(cp)

    row = lax.broadcasted_iota(jnp.int32, (tile, chans), 0)
    for b in range(3):
        x = gpad[h + 2 - b].astype(F32)
        ahead = jnp.where(lax.rem(row, columns) == columns - 1, 0.0, pltpu.roll(x, tile - 1, 0))
        behind = jnp.where(lax.rem(row, columns) == 0, 0.0, pltpu.roll(x, 1, 0))
        for j, y in enumerate((ahead, x, behind)):
            win[3 * b + j] = y.astype(BF16)
    loads[2].wait()

    def taps(a):
        acc = mm_nt(win[0], wconv[9 * a])
        for i in range(1, 9):
            acc = acc + mm_nt(win[i], wconv[9 * a + i])
        return acc

    y0, y1 = taps(0), taps(1)
    cut = columns
    ig_send[...] = jnp.concatenate([y0[:cut], y0[cut:] + y1[:cut]], 0).astype(BF16)

    def to_prev():
        return remote(ig_send, ig_got, is_sem, ir_sem, (jnp.maximum(t - 1, 0), h, c))

    @pl.when(t > 0)
    def _():
        to_prev().start()

    @pl.when(t == n_t - 1)
    def _():
        ig_got[...] = jnp.zeros_like(ig_got)

    acc = part_f[pl.ds(c * ht, ht)]
    for k in range(1, n_b):
        peer = lax.rem(c + k, n_b)
        remote(part_b.at[pl.ds(0, ht)], got1.at[peer], s1s.at[k], s1r.at[peer], (t, h, peer)).wait_recv()
        acc = acc + got1[peer].astype(F32)
    half_f[...] = acc
    half_b[...] = acc.astype(BF16)
    for k in range(1, n_t):
        peer = lax.rem(t + k, n_t)
        cp = remote(half_b.at[pl.ds(peer * tp, tp)], got2.at[t], s2s.at[k], s2r.at[t], (peer, h, c))
        cp.start()
        sends.append(cp)

    y2 = taps(2)
    own_ig = y2 + jnp.concatenate([y1[cut:], jnp.zeros((tile - cut, chans), F32)], 0)

    acc = half_f[pl.ds(t * tp, tp)]
    for k in range(1, n_t):
        peer = lax.rem(t + k, n_t)
        remote(half_b.at[pl.ds(0, tp)], got2.at[peer], s2s.at[k], s2r.at[peer], (peer, h, c)).wait_recv()
        acc = acc + got2[peer].astype(F32)
    total[c, t] = acc.astype(BF16)

    for k in range(1, n_t):
        peer = lax.rem(t + k, n_t)
        cp = remote(total.at[c, t], total.at[c, t], s3s.at[k], s3r.at[t], (peer, h, c))
        cp.start()
        sends.append(cp)

    def across(piece, k):
        return remote(
            total.at[c, piece], total.at[c, piece], s4s.at[piece, k], s4r.at[c, piece],
            (t, h, lax.rem(c + k, n_b)),
        )

    for k in range(1, n_b):
        cp = across(t, k)
        cp.start()
        sends.append(cp)

    @pl.when(t < n_t - 1)
    def _():
        to_prev().wait_recv()

    igrad_ref[...] = (own_ig + ig_got[...].astype(F32)).astype(BF16)

    for m in range(1, n_t):
        peer = lax.rem(t + m, n_t)
        remote(total.at[c, peer], total.at[c, peer], s3s.at[m], s3r.at[peer], (peer, h, c)).wait_recv()
        for k in range(1, n_b):
            cp = across(peer, k)
            cp.start()
            sends.append(cp)
    for m in range(n_t):
        piece = lax.rem(t + m, n_t)
        for k in range(1, n_b):
            peer = lax.rem(c + k, n_b)
            remote(
                total.at[peer, piece], total.at[peer, piece], s4s.at[piece, k], s4r.at[peer, piece],
                (t, h, peer),
            ).wait_recv()
    wgrad_ref[...] = total[...].reshape(n_b * ht, dblk, chans)

    for cp in sends:
        cp.wait_send()

    @pl.when(t < n_t - 1)
    def _():
        for k in range(n_h):
            to_next(k).wait_send()

    @pl.when(t > 0)
    def _():
        to_prev().wait_send()


def local(conv_input, saved, cotangent, gain, w_conv, w_qkv, w_out):
    chans = saved.shape[-1]
    frames, columns = saved.shape[1], saved.shape[2] * saved.shape[3]
    n_t, n_h, n_b = (lax.axis_size(x) for x in ("tm", "height", "batch"))
    tile = frames * columns
    dblk = chans // n_h
    tp = -(-27 // (n_t * n_b))
    ht = n_t * tp
    taps = n_b * ht
    sizes = (n_t, n_h, n_b, frames, columns, chans, tp)
    vmem = pl.BlockSpec(memory_space=pltpu.VMEM)
    hbm = pl.BlockSpec(memory_space=pl.ANY)
    dma = pltpu.SemaphoreType.DMA
    igrad, wgrad = pl.pallas_call(
        functools.partial(body, sizes),
        out_shape=(
            jax.ShapeDtypeStruct((tile, chans), BF16),
            jax.ShapeDtypeStruct((taps, dblk, chans), BF16),
        ),
        in_specs=[vmem] * 4 + [hbm] * 3,
        out_specs=(vmem, vmem),
        scratch_shapes=[
            pltpu.VMEM((chans, 3 * chans), BF16),
            pltpu.VMEM((chans, chans), BF16),
            pltpu.VMEM((27, chans, chans), BF16),
            pltpu.VMEM((2, n_h, tile, chans), BF16),
            pltpu.VMEM((n_h, dblk, tile), BF16),
            pltpu.VMEM((2, n_h, dblk, tile), BF16),
            pltpu.VMEM((n_h + 2, tile, chans), BF16),
            pltpu.VMEM((9, n_h + 2, dblk, tile), BF16),
            pltpu.VMEM((9, tile, chans), BF16),
            pltpu.VMEM((taps, dblk, chans), F32),
            pltpu.VMEM((taps, dblk, chans), BF16),
            pltpu.VMEM((ht, dblk, chans), F32),
            pltpu.VMEM((ht, dblk, chans), BF16),
            pltpu.VMEM((n_b, ht, dblk, chans), BF16),
            pltpu.VMEM((n_t, tp, dblk, chans), BF16),
            pltpu.VMEM((n_b, n_t, tp, dblk, chans), BF16),
            pltpu.VMEM((tile, chans), BF16),
            pltpu.VMEM((tile, chans), BF16),
            dma((3,)), dma((2, n_h)), dma((2, n_h)), dma((2, n_h)), dma((2, n_h)), dma, dma,
            dma((n_b,)), dma((n_b,)), dma((n_t,)), dma((n_t,)), dma((n_t,)), dma((n_t,)),
            dma((n_t, n_b)), dma((n_b, n_t)),
        ],
        compiler_params=pltpu.CompilerParams(
            collective_id=0, has_side_effects=True, vmem_limit_bytes=56 * 1024 * 1024
        ),
    )(
        saved.reshape(tile, chans), cotangent.reshape(tile, chans), conv_input.reshape(tile, chans),
        gain.reshape(1, chans), w_qkv, w_out, w_conv.reshape(27, chans, chans),
    )
    weight_grad = wgrad[:27].astype(F32).transpose(1, 0, 2)
    return igrad.reshape(conv_input.shape), weight_grad


def solution(mesh):
    banded = P("batch", "tm", "height", None, None)
    return jax.shard_map(
        local,
        mesh=mesh,
        in_specs=(banded, banded, banded, P(), P(), P(), P()),
        out_specs=(banded, P("height", None, None)),
        check_vma=False,
    )
```

```python
import functools
import math

import jax
import jax.numpy as jnp
from jax import lax
from jax.experimental import pallas as pl
from jax.experimental.pallas import tpu as pltpu
from jax.sharding import PartitionSpec as P

EPS = 1e-06
NT = (((1,), (1,)), ((), ()))
TN = (((0,), (0,)), ((), ()))
F32 = jnp.float32
BF16 = jnp.bfloat16


def mm(x, y):
    return jnp.dot(x, y, preferred_element_type=F32)


def mm_nt(x, y):
    return lax.dot_general(x, y, NT, preferred_element_type=F32)


def mm_tn(x, y):
    return lax.dot_general(x, y, TN, preferred_element_type=F32)


def body(
    sizes,
    saved_ref, cot_ref, conv_ref, gain_ref, wqkv_hbm, wout_hbm, wconv_hbm,
    igrad_ref, wgrad_ref,
    wqkv, wout, wconv, xall, conv_t, recv_t, gpad, lhs, win,
    part_f, part_b, half_f, half_b, got1, got2, total, ig_send, ig_got,
    wsem, gs_sem, gr_sem, cs_sem, cr_sem, is_sem, ir_sem,
    s1s, s1r, s2s, s2r, s3s, s3r, s4s, s4r,
):
    n_t, n_h, n_b, frames, columns, chans, tp = sizes
    tile = frames * columns
    dblk = chans // n_h
    n_a = n_h // 2
    ht = n_t * tp
    t = lax.axis_index("tm")
    h = lax.axis_index("height")
    c = lax.axis_index("batch")
    scale = 1.0 / math.sqrt(chans)
    norm = 1.0 / math.sqrt(n_b * n_t * frames * n_h * columns)

    loads = [
        pltpu.make_async_copy(wqkv_hbm, wqkv, wsem.at[0]),
        pltpu.make_async_copy(wout_hbm, wout, wsem.at[1]),
        pltpu.make_async_copy(wconv_hbm, wconv, wsem.at[2]),
    ]
    for load in loads:
        load.start()

    def remote(src, dst, ssem, rsem, dev):
        return pltpu.make_async_remote_copy(
            src_ref=src, dst_ref=dst, send_sem=ssem, recv_sem=rsem,
            device_id=dev, device_id_type=pl.DeviceIdType.MESH,
        )

    barrier = pltpu.get_barrier_semaphore()
    for dt in range(n_t):
        for dh in range(n_h):
            if dt or dh:
                pl.semaphore_signal(
                    barrier, inc=1,
                    device_id=(lax.rem(t + dt, n_t), lax.rem(h + dh, n_h), c),
                    device_id_type=pl.DeviceIdType.MESH,
                )
    for db in range(1, n_b):
        pl.semaphore_signal(
            barrier, inc=1, device_id=(t, h, lax.rem(c + db, n_b)),
            device_id_type=pl.DeviceIdType.MESH,
        )
    pl.semaphore_wait(barrier, n_t * n_h - 1 + n_b - 1)

    h_a, h_b = h // 2, lax.rem(h, 2)
    mate = h_a * 2 + (1 - h_b)
    order = sorted(range(1, n_a), key=lambda k: min(k, n_a - k))
    sends = []
    mine = (saved_ref, cot_ref)

    def block(f, arr, src, slot, dev, own=False):
        rows = pl.ds(f * columns, columns)
        dst = xall.at[arr, src, rows]
        return remote(
            mine[arr].at[rows] if own else dst, dst,
            gs_sem.at[2 * f + arr, slot], gr_sem.at[2 * f + arr, src], (t, dev, c),
        )

    def send_own(f):
        for arr in range(2):
            for k in order:
                cp = block(f, arr, h, k, lax.rem(h_a + k, n_a) * 2 + h_b, True)
                cp.start()
                sends.append(cp)
            cp = block(f, arr, h, 0, mate, True)
            cp.start()
            sends.append(cp)

    def pass_on(f, arr, k):
        src = lax.rem(h_a + k, n_a) * 2 + h_b
        block(f, arr, src, k, mate).wait_recv()
        cp = block(f, arr, src, n_a + k - 1, mate)
        cp.start()
        sends.append(cp)

    def arrived(f, arr):
        for k in range(n_a):
            src = lax.rem(h_a + k, n_a) * 2 + (1 - h_b)
            block(f, arr, src, 0, mate).wait_recv()

    send_own(0)
    for arr in range(2):
        xall[arr, h] = mine[arr][...]

    flipped = conv_ref[...].astype(F32).T.astype(BF16)
    for k in range(n_h):
        conv_t[k] = flipped[k * dblk:(k + 1) * dblk]
    recv_t[0, h] = conv_t[h]

    for arr in range(2):
        for k in order:
            pass_on(0, arr, k)
    for f in range(1, frames):
        send_own(f)

    for k in range(1, n_h):
        peer = lax.rem(h + k, n_h)
        cp = remote(conv_t.at[peer], recv_t.at[0, h], cs_sem.at[0, k], cr_sem.at[0, h], (t, peer, c))
        cp.start()
        sends.append(cp)

    def to_next(k):
        peer = lax.rem(h + k, n_h)
        later = jnp.minimum(t + 1, n_t - 1)
        return remote(conv_t.at[peer], recv_t.at[1, h], cs_sem.at[1, k], cr_sem.at[1, h], (later, peer, c))

    @pl.when(t < n_t - 1)
    def _():
        for k in range(n_h):
            to_next(k).start()

    @pl.when(t == 0)
    def _():
        recv_t[1] = jnp.zeros_like(recv_t[1])

    loads[0].wait()
    loads[1].wait()
    gain = gain_ref[...]
    keys_n = n_h * columns
    gpad[0] = jnp.zeros_like(gpad[0])
    gpad[n_h + 1] = jnp.zeros_like(gpad[0])

    for f in range(frames):
        rows = pl.ds(f * columns, columns)
        coming = [(f + 1, arr, k) for arr in range(2) for k in order] if f + 1 < frames else []
        arrived(f, 0)
        hidden = xall[0, :, rows, :].reshape(keys_n, chans).astype(F32)
        inverse = lax.rsqrt(jnp.mean(hidden * hidden, -1, keepdims=True) + EPS)
        normed = (hidden * inverse * gain).astype(BF16)
        qkv = mm(normed, wqkv[...]).astype(BF16)
        q, k, v = qkv[:, :chans], qkv[:, chans:2 * chans], qkv[:, 2 * chans:]
        s = mm_nt(k, q) * scale
        e = jnp.exp(s - jnp.max(s, 0, keepdims=True))
        p = e / jnp.sum(e, 0, keepdims=True)
        arrived(f, 1)
        for item in coming[:len(order) // 2]:
            pass_on(*item)
        cot = xall[1, :, rows, :].reshape(keys_n, chans)
        go = mm_nt(cot, wout[...]).astype(BF16)
        gp = mm_nt(v, go)
        delta = jnp.sum(p * gp, 0, keepdims=True)
        gs = (p * (gp - delta) * scale).astype(BF16)
        gq = mm_tn(gs, k).astype(BF16)
        gk = mm(gs, q).astype(BF16)
        gv = mm(p.astype(BF16), go).astype(BF16)
        for item in coming[len(order) // 2:len(order)]:
            pass_on(*item)
        gn = (
            mm_nt(gq, wqkv[:, :chans])
            + mm_nt(gk, wqkv[:, chans:2 * chans])
            + mm_nt(gv, wqkv[:, 2 * chans:])
        )
        scaled = gn * gain
        g = cot.astype(F32) + inverse * (
            scaled - hidden * inverse * inverse * jnp.mean(scaled * hidden, -1, keepdims=True)
        )
        gpad[1:n_h + 1, rows, :] = g.astype(BF16).reshape(n_h, columns, chans)
        for item in coming[len(order):]:
            pass_on(*item)

    for k in range(1, n_h):
        src = lax.rem(h + k, n_h)
        remote(conv_t.at[0], recv_t.at[0, src], cs_sem.at[0, k], cr_sem.at[0, src], (t, src, c)).wait_recv()

    @pl.when(t > 0)
    def _():
        for k in range(n_h):
            src = lax.rem(h + k, n_h)
            remote(conv_t.at[0], recv_t.at[1, src], cs_sem.at[1, k], cr_sem.at[1, src], (t, mate, c)).wait_recv()

    lane = lax.broadcasted_iota(jnp.int32, (dblk, tile), 1)
    for a in range(3):
        for j in range(3):
            lhs[3 * a + j, 0] = jnp.zeros((dblk, tile), BF16)
            lhs[3 * a + j, n_h + 1] = jnp.zeros((dblk, tile), BF16)

    def shifts(r, carry):
        own = recv_t[0, r].astype(F32)
        prev = recv_t[1, r].astype(F32)
        both = jnp.where(lane < columns, pltpu.roll(prev, columns, 1), pltpu.roll(own, columns, 1))
        for a, x in enumerate((prev, both, own)):
            left = jnp.where(lax.rem(lane, columns) == 0, 0.0, pltpu.roll(x, 1, 1))
            right = jnp.where(lax.rem(lane, columns) == columns - 1, 0.0, pltpu.roll(x, tile - 1, 1))
            for j, y in enumerate((left, x, right)):
                lhs[3 * a + j, r + 1] = y.astype(BF16)
        return carry

    lax.fori_loop(0, n_h, shifts, 0)

    for tap in range(27, n_b * ht):
        part_f[tap] = jnp.zeros((dblk, chans), F32)
        part_b[tap] = jnp.zeros((dblk, chans), BF16)
    rights = gpad[1:n_h + 1].reshape(n_h * tile, chans)
    halves = [
        remote(
            part_b.at[pl.ds(lax.rem(c + k, n_b) * ht, ht)], got1.at[c], s1s.at[k], s1r.at[c],
            (t, h, lax.rem(c + k, n_b)),
        )
        for k in range(1, n_b)
    ]
    sends += halves
    for i in range(3):
        b = jnp.where(c == 0, 2 - i, i)
        left = jnp.concatenate(
            [lhs[:, b + r].reshape(9 * dblk, tile) for r in range(n_h)], axis=1
        )
        out = (mm(left, rights) * norm).reshape(9, dblk, chans)
        part_f[pl.ds(9 * b, 9)] = out
        part_b[pl.ds(9 * b, 9)] = out.astype(BF16)
        if i == (1 if n_b == 2 and ht <= 18 else 2):
            for cp in halves:
                cp.start()

    row = lax.broadcasted_iota(jnp.int32, (tile, chans), 0)
    for b in range(3):
        x = gpad[h + 2 - b].astype(F32)
        ahead = jnp.where(lax.rem(row, columns) == columns - 1, 0.0, pltpu.roll(x, tile - 1, 0))
        behind = jnp.where(lax.rem(row, columns) == 0, 0.0, pltpu.roll(x, 1, 0))
        for j, y in enumerate((ahead, x, behind)):
            win[3 * b + j] = y.astype(BF16)
    loads[2].wait()

    def taps(a):
        acc = mm_nt(win[0], wconv[9 * a])
        for i in range(1, 9):
            acc = acc + mm_nt(win[i], wconv[9 * a + i])
        return acc

    y0 = taps(0)
    acc = part_f[pl.ds(c * ht, ht)]
    for k in range(1, n_b):
        peer = lax.rem(c + k, n_b)
        remote(part_b.at[pl.ds(0, ht)], got1.at[peer], s1s.at[k], s1r.at[peer], (t, h, peer)).wait_recv()
        acc = acc + got1[peer].astype(F32)
    half_f[...] = acc
    half_b[...] = acc.astype(BF16)
    for k in range(1, n_t):
        peer = lax.rem(t + k, n_t)
        cp = remote(half_b.at[pl.ds(peer * tp, tp)], got2.at[t], s2s.at[k], s2r.at[t], (peer, h, c))
        cp.start()
        sends.append(cp)

    y1 = taps(1)
    cut = columns
    ig_send[...] = jnp.concatenate([y0[:cut], y0[cut:] + y1[:cut]], 0).astype(BF16)

    def to_prev():
        return remote(ig_send, ig_got, is_sem, ir_sem, (jnp.maximum(t - 1, 0), h, c))

    @pl.when(t > 0)
    def _():
        to_prev().start()

    @pl.when(t == n_t - 1)
    def _():
        ig_got[...] = jnp.zeros_like(ig_got)

    y2 = taps(2)
    own_ig = y2 + jnp.concatenate([y1[cut:], jnp.zeros((tile - cut, chans), F32)], 0)

    acc = half_f[pl.ds(t * tp, tp)]
    for k in range(1, n_t):
        peer = lax.rem(t + k, n_t)
        remote(half_b.at[pl.ds(0, tp)], got2.at[peer], s2s.at[k], s2r.at[peer], (peer, h, c)).wait_recv()
        acc = acc + got2[peer].astype(F32)
    total[c, t] = acc.astype(BF16)

    for k in range(1, n_t):
        peer = lax.rem(t + k, n_t)
        cp = remote(total.at[c, t], total.at[c, t], s3s.at[k], s3r.at[t], (peer, h, c))
        cp.start()
        sends.append(cp)

    def across(piece, k):
        return remote(
            total.at[c, piece], total.at[c, piece], s4s.at[piece, k], s4r.at[c, piece],
            (t, h, lax.rem(c + k, n_b)),
        )

    for k in range(1, n_b):
        cp = across(t, k)
        cp.start()
        sends.append(cp)

    @pl.when(t < n_t - 1)
    def _():
        to_prev().wait_recv()

    igrad_ref[...] = (own_ig + ig_got[...].astype(F32)).astype(BF16)

    for m in range(1, n_t):
        peer = lax.rem(t + m, n_t)
        remote(total.at[c, peer], total.at[c, peer], s3s.at[m], s3r.at[peer], (peer, h, c)).wait_recv()
        for k in range(1, n_b):
            cp = across(peer, k)
            cp.start()
            sends.append(cp)
    for m in range(n_t):
        piece = lax.rem(t + m, n_t)
        for k in range(1, n_b):
            peer = lax.rem(c + k, n_b)
            remote(
                total.at[peer, piece], total.at[peer, piece], s4s.at[piece, k], s4r.at[peer, piece],
                (t, h, peer),
            ).wait_recv()
    whole = total.reshape(n_b * ht, dblk, chans)
    for a in range(3):
        for b in range(3):
            wgrad_ref[9 * a + 3 * b:9 * a + 3 * b + 3] = whole[9 * b + 3 * a:9 * b + 3 * a + 3]

    for cp in sends:
        cp.wait_send()

    @pl.when(t < n_t - 1)
    def _():
        for k in range(n_h):
            to_next(k).wait_send()

    @pl.when(t > 0)
    def _():
        to_prev().wait_send()


def local(conv_input, saved, cotangent, gain, w_conv, w_qkv, w_out):
    chans = saved.shape[-1]
    frames, columns = saved.shape[1], saved.shape[2] * saved.shape[3]
    n_t, n_h, n_b = (lax.axis_size(x) for x in ("tm", "height", "batch"))
    tile = frames * columns
    dblk = chans // n_h
    tp = -(-27 // (n_t * n_b))
    ht = n_t * tp
    taps = n_b * ht
    sizes = (n_t, n_h, n_b, frames, columns, chans, tp)
    vmem = pl.BlockSpec(memory_space=pltpu.VMEM)
    hbm = pl.BlockSpec(memory_space=pl.ANY)
    dma = pltpu.SemaphoreType.DMA
    igrad, wgrad = pl.pallas_call(
        functools.partial(body, sizes),
        out_shape=(
            jax.ShapeDtypeStruct((tile, chans), BF16),
            jax.ShapeDtypeStruct((27, dblk, chans), BF16),
        ),
        in_specs=[vmem] * 4 + [hbm] * 3,
        out_specs=(vmem, vmem),
        scratch_shapes=[
            pltpu.VMEM((chans, 3 * chans), BF16),
            pltpu.VMEM((chans, chans), BF16),
            pltpu.VMEM((27, chans, chans), BF16),
            pltpu.VMEM((2, n_h, tile, chans), BF16),
            pltpu.VMEM((n_h, dblk, tile), BF16),
            pltpu.VMEM((2, n_h, dblk, tile), BF16),
            pltpu.VMEM((n_h + 2, tile, chans), BF16),
            pltpu.VMEM((9, n_h + 2, dblk, tile), BF16),
            pltpu.VMEM((9, tile, chans), BF16),
            pltpu.VMEM((taps, dblk, chans), F32),
            pltpu.VMEM((taps, dblk, chans), BF16),
            pltpu.VMEM((ht, dblk, chans), F32),
            pltpu.VMEM((ht, dblk, chans), BF16),
            pltpu.VMEM((n_b, ht, dblk, chans), BF16),
            pltpu.VMEM((n_t, tp, dblk, chans), BF16),
            pltpu.VMEM((n_b, n_t, tp, dblk, chans), BF16),
            pltpu.VMEM((tile, chans), BF16),
            pltpu.VMEM((tile, chans), BF16),
            dma((3,)), dma((2 * frames, n_h)), dma((2 * frames, n_h)), dma((2, n_h)), dma((2, n_h)), dma, dma,
            dma((n_b,)), dma((n_b,)), dma((n_t,)), dma((n_t,)), dma((n_t,)), dma((n_t,)),
            dma((n_t, n_b)), dma((n_b, n_t)),
        ],
        compiler_params=pltpu.CompilerParams(
            collective_id=0, has_side_effects=True, vmem_limit_bytes=56 * 1024 * 1024
        ),
    )(
        saved.reshape(tile, chans), cotangent.reshape(tile, chans), conv_input.reshape(tile, chans),
        gain.reshape(1, chans), w_qkv, w_out, w_conv.reshape(27, chans, chans),
    )
    weight_grad = wgrad.astype(F32).transpose(1, 0, 2)
    return igrad.reshape(conv_input.shape), weight_grad


def solution(mesh):
    banded = P("batch", "tm", "height", None, None)
    return jax.shard_map(
        local,
        mesh=mesh,
        in_specs=(banded, banded, banded, P(), P(), P(), P()),
        out_specs=(banded, P("height", None, None)),
        check_vma=False,
    )
```

```python
import functools
import math

import jax
import jax.numpy as jnp
from jax import lax
from jax.experimental import pallas as pl
from jax.experimental.pallas import tpu as pltpu
from jax.sharding import PartitionSpec as P

EPS = 1e-06
NT = (((1,), (1,)), ((), ()))
TN = (((0,), (0,)), ((), ()))
F32 = jnp.float32
BF16 = jnp.bfloat16


def mm(x, y):
    return jnp.dot(x, y, preferred_element_type=F32)


def mm_nt(x, y):
    return lax.dot_general(x, y, NT, preferred_element_type=F32)


def mm_tn(x, y):
    return lax.dot_general(x, y, TN, preferred_element_type=F32)


def body(
    sizes,
    saved_ref, cot_ref, conv_ref, gain_ref, wqkv_hbm, wout_hbm, wconv_hbm,
    igrad_ref, wgrad_ref,
    wqkv, wout, wconv, xall, conv_t, recv_t, gpad, gall, lhs, win,
    part_f, part_b, got1, total, ig_send, ig_got,
    wsem, gs_sem, gr_sem, cs_sem, cr_sem, xs_sem, xr_sem, is_sem, ir_sem,
    s1s, s1r, s4s, s4r,
):
    n_t, n_h, n_b, frames, columns, chans, ht = sizes
    tile = frames * columns
    dblk = chans // n_h
    n_a = n_h // 2
    t = lax.axis_index("tm")
    h = lax.axis_index("height")
    c = lax.axis_index("batch")
    scale = 1.0 / math.sqrt(chans)
    norm = 1.0 / math.sqrt(n_b * n_t * frames * n_h * columns)

    loads = [
        pltpu.make_async_copy(wqkv_hbm, wqkv, wsem.at[0]),
        pltpu.make_async_copy(wout_hbm, wout, wsem.at[1]),
        pltpu.make_async_copy(wconv_hbm, wconv, wsem.at[2]),
    ]
    for load in loads:
        load.start()

    def remote(src, dst, ssem, rsem, dev):
        return pltpu.make_async_remote_copy(
            src_ref=src, dst_ref=dst, send_sem=ssem, recv_sem=rsem,
            device_id=dev, device_id_type=pl.DeviceIdType.MESH,
        )

    barrier = pltpu.get_barrier_semaphore()
    for dt in range(n_t):
        for dh in range(n_h):
            if dt or dh:
                pl.semaphore_signal(
                    barrier, inc=1,
                    device_id=(lax.rem(t + dt, n_t), lax.rem(h + dh, n_h), c),
                    device_id_type=pl.DeviceIdType.MESH,
                )
    for db in range(1, n_b):
        pl.semaphore_signal(
            barrier, inc=1, device_id=(t, h, lax.rem(c + db, n_b)),
            device_id_type=pl.DeviceIdType.MESH,
        )
    pl.semaphore_wait(barrier, n_t * n_h - 1 + n_b - 1)

    h_a, h_b = h // 2, lax.rem(h, 2)
    mate = h_a * 2 + (1 - h_b)
    order = sorted(range(1, n_a), key=lambda k: min(k, n_a - k))
    sends = []
    mine = (saved_ref, cot_ref)

    def block(f, arr, src, slot, dev, own=False):
        rows = pl.ds(f * columns, columns)
        dst = xall.at[arr, src, rows]
        return remote(
            mine[arr].at[rows] if own else dst, dst,
            gs_sem.at[2 * f + arr, slot], gr_sem.at[2 * f + arr, src], (t, dev, c),
        )

    def send_own(f):
        for arr in range(2):
            for k in order:
                cp = block(f, arr, h, k, lax.rem(h_a + k, n_a) * 2 + h_b, True)
                cp.start()
                sends.append(cp)
            cp = block(f, arr, h, 0, mate, True)
            cp.start()
            sends.append(cp)

    def pass_on(f, arr, k):
        src = lax.rem(h_a + k, n_a) * 2 + h_b
        block(f, arr, src, k, mate).wait_recv()
        cp = block(f, arr, src, n_a + k - 1, mate)
        cp.start()
        sends.append(cp)

    def arrived(f, arr):
        for k in range(n_a):
            src = lax.rem(h_a + k, n_a) * 2 + (1 - h_b)
            block(f, arr, src, 0, mate).wait_recv()

    send_own(0)
    for arr in range(2):
        xall[arr, h] = mine[arr][...]

    flipped = conv_ref[...].astype(F32).T.astype(BF16)
    for k in range(n_h):
        conv_t[k] = flipped[k * dblk:(k + 1) * dblk]
    recv_t[t, h] = conv_t[h]

    for arr in range(2):
        for k in order:
            pass_on(0, arr, k)
    for f in range(1, frames):
        send_own(f)

    for m in range(n_t):
        for k in range(n_h):
            if m or k:
                dt, peer = lax.rem(t + m, n_t), lax.rem(h + k, n_h)
                cp = remote(conv_t.at[peer], recv_t.at[t, h], cs_sem.at[m, k], cr_sem.at[t, h], (dt, peer, c))
                cp.start()
                sends.append(cp)

    def across_tm(f, m, j):
        rows = pl.ds(f * columns, columns)
        src = 2 * j + h_b
        return remote(
            gpad.at[1 + src, rows], gall.at[t, src, rows],
            xs_sem.at[f * n_t + m, j], xr_sem.at[f * n_t + t, src], (lax.rem(t + m, n_t), h, c),
        )

    def to_mate(f, m, j, parity):
        rows = pl.ds(f * columns, columns)
        frm, src = lax.rem(t + m, n_t), 2 * j + parity
        return remote(
            gall.at[frm, src, rows], gall.at[frm, src, rows],
            xs_sem.at[f * n_t + m, n_a + j], xr_sem.at[f * n_t + frm, src], (t, mate, c),
        )

    def relay(f, j):
        for m in range(1, n_t):
            cp = to_mate(f, m, j, h_b)
            cp.wait_recv()
            cp.start()
            sends.append(cp)

    loads[0].wait()
    loads[1].wait()
    gain = gain_ref[...]
    keys_n = n_h * columns
    gpad[0] = jnp.zeros_like(gpad[0])
    gpad[n_h + 1] = jnp.zeros_like(gpad[0])

    for f in range(frames):
        rows = pl.ds(f * columns, columns)
        coming = [(f + 1, arr, k) for arr in range(2) for k in order] if f + 1 < frames else []
        arrived(f, 0)
        hidden = xall[0, :, rows, :].reshape(keys_n, chans).astype(F32)
        inverse = lax.rsqrt(jnp.mean(hidden * hidden, -1, keepdims=True) + EPS)
        normed = (hidden * inverse * gain).astype(BF16)
        qkv = mm(normed, wqkv[...]).astype(BF16)
        q, k, v = qkv[:, :chans], qkv[:, chans:2 * chans], qkv[:, 2 * chans:]
        s = mm_nt(k, q) * scale
        e = jnp.exp(s - jnp.max(s, 0, keepdims=True))
        p = e / jnp.sum(e, 0, keepdims=True)
        arrived(f, 1)
        for item in coming[:len(order) // 2]:
            pass_on(*item)
        cot = xall[1, :, rows, :].reshape(keys_n, chans)
        go = mm_nt(cot, wout[...]).astype(BF16)
        gp = mm_nt(v, go)
        delta = jnp.sum(p * gp, 0, keepdims=True)
        gs = (p * (gp - delta) * scale).astype(BF16)
        gq = mm_tn(gs, k).astype(BF16)
        gk = mm(gs, q).astype(BF16)
        gv = mm(p.astype(BF16), go).astype(BF16)
        for item in coming[len(order) // 2:len(order)]:
            pass_on(*item)
        gn = (
            mm_nt(gq, wqkv[:, :chans])
            + mm_nt(gk, wqkv[:, chans:2 * chans])
            + mm_nt(gv, wqkv[:, 2 * chans:])
        )
        scaled = gn * gain
        g = cot.astype(F32) + inverse * (
            scaled - hidden * inverse * inverse * jnp.mean(scaled * hidden, -1, keepdims=True)
        )
        gpad[1:n_h + 1, rows, :] = g.astype(BF16).reshape(n_h, columns, chans)
        for j in range(n_a):
            for m in range(1, n_t):
                cp = across_tm(f, m, j)
                cp.start()
                sends.append(cp)
        for item in coming[len(order):]:
            pass_on(*item)

    for m in range(n_t):
        for k in range(n_h):
            if m or k:
                frm, src = lax.rem(t + m, n_t), lax.rem(h + k, n_h)
                remote(conv_t.at[0], recv_t.at[frm, src], cs_sem.at[m, k], cr_sem.at[frm, src], (frm, src, c)).wait_recv()

    for f in range(frames - 1):
        for j in range(n_a):
            relay(f, j)

    lane = lax.broadcasted_iota(jnp.int32, (dblk, tile), 1)
    for m in range(n_t):
        for i in range(9):
            lhs[m, i, 0] = jnp.zeros((dblk, tile), BF16)
            lhs[m, i, n_h + 1] = jnp.zeros((dblk, tile), BF16)

    def build(m):
        frm = lax.rem(t + m, n_t)
        before = jnp.maximum(frm - 1, 0)

        def shifts(r, carry):
            own = recv_t[frm, r].astype(F32)
            prev = jnp.where(frm > 0, recv_t[before, r].astype(F32), 0.0)
            both = jnp.where(lane < columns, pltpu.roll(prev, columns, 1), pltpu.roll(own, columns, 1))
            for a, x in enumerate((prev, both, own)):
                left = jnp.where(lax.rem(lane, columns) == 0, 0.0, pltpu.roll(x, 1, 1))
                right = jnp.where(lax.rem(lane, columns) == columns - 1, 0.0, pltpu.roll(x, tile - 1, 1))
                for j, y in enumerate((left, x, right)):
                    lhs[m, 3 * a + j, r + 1] = y.astype(BF16)
            return carry

        lax.fori_loop(0, n_h, shifts, 0)

    def product(m, b, rights):
        left = jnp.concatenate(
            [lhs[m, :, b + r].reshape(9 * dblk, tile) for r in range(n_h)], axis=1
        )
        return mm(left, rights).reshape(9, dblk, chans)

    build(0)
    for tap in range(27, n_b * ht):
        part_f[tap] = jnp.zeros((dblk, chans), F32)
        part_b[tap] = jnp.zeros((dblk, chans), BF16)
    rights = gpad[1:n_h + 1].reshape(n_h * tile, chans)
    spots = [(j * 3) // n_a for j in range(n_a)]
    for b in range(3):
        part_f[9 * b:9 * b + 9] = product(0, b, rights)
        for j in range(n_a - 1):
            if spots[j] == b:
                relay(frames - 1, j)
    for j in range(n_a - 1):
        if spots[j] > 2:
            relay(frames - 1, j)

    row = lax.broadcasted_iota(jnp.int32, (tile, chans), 0)
    for b in range(3):
        x = gpad[h + 2 - b].astype(F32)
        ahead = jnp.where(lax.rem(row, columns) == columns - 1, 0.0, pltpu.roll(x, tile - 1, 0))
        behind = jnp.where(lax.rem(row, columns) == 0, 0.0, pltpu.roll(x, 1, 0))
        for j, y in enumerate((ahead, x, behind)):
            win[3 * b + j] = y.astype(BF16)
    loads[2].wait()

    def taps(a):
        acc = mm_nt(win[0], wconv[9 * a])
        for i in range(1, 9):
            acc = acc + mm_nt(win[i], wconv[9 * a + i])
        return acc

    y0 = taps(0)
    relay(frames - 1, n_a - 1)
    y1 = taps(1)
    cut = columns
    ig_send[...] = jnp.concatenate([y0[:cut], y0[cut:] + y1[:cut]], 0).astype(BF16)

    def to_prev():
        return remote(ig_send, ig_got, is_sem, ir_sem, (jnp.maximum(t - 1, 0), h, c))

    @pl.when(t > 0)
    def _():
        to_prev().start()

    @pl.when(t == n_t - 1)
    def _():
        ig_got[...] = jnp.zeros_like(ig_got)

    y2 = taps(2)
    own_ig = y2 + jnp.concatenate([y1[cut:], jnp.zeros((tile - cut, chans), F32)], 0)
    for m in range(1, n_t):
        build(m)

    halves = [
        remote(
            part_b.at[pl.ds(lax.rem(c + k, n_b) * ht, ht)], got1.at[c], s1s.at[k], s1r.at[c],
            (t, h, lax.rem(c + k, n_b)),
        )
        for k in range(1, n_b)
    ]
    sends += halves
    for m in range(1, n_t):
        for f in range(frames):
            for j in range(n_a):
                to_mate(f, m, j, 1 - h_b).wait_recv()
    for m in range(1, max(n_t, 2)):
        rights = gall[lax.rem(t + m, n_t)].reshape(n_h * tile, chans)
        for i in range(3):
            b = jnp.where(c == 0, 2 - i, i)
            out = part_f[pl.ds(9 * b, 9)]
            if n_t > 1:
                out = out + product(m, b, rights)
            if m == max(n_t, 2) - 1:
                out = out * norm
                part_b[pl.ds(9 * b, 9)] = out.astype(BF16)
            part_f[pl.ds(9 * b, 9)] = out
            if m == max(n_t, 2) - 1 and i == (1 if n_b == 2 and ht <= 18 else 2):
                for cp in halves:
                    cp.start()

    acc = part_f[pl.ds(c * ht, ht)]
    for k in range(1, n_b):
        peer = lax.rem(c + k, n_b)
        remote(part_b.at[pl.ds(0, ht)], got1.at[peer], s1s.at[k], s1r.at[peer], (t, h, peer)).wait_recv()
        acc = acc + got1[peer].astype(F32)
    total[c] = acc.astype(BF16)
    for k in range(1, n_b):
        cp = remote(total.at[c], total.at[c], s4s.at[k], s4r.at[c], (t, h, lax.rem(c + k, n_b)))
        cp.start()
        sends.append(cp)

    @pl.when(t < n_t - 1)
    def _():
        to_prev().wait_recv()

    igrad_ref[...] = (own_ig + ig_got[...].astype(F32)).astype(BF16)

    for k in range(1, n_b):
        peer = lax.rem(c + k, n_b)
        remote(total.at[peer], total.at[peer], s4s.at[k], s4r.at[peer], (t, h, peer)).wait_recv()
    whole = total.reshape(n_b * ht, dblk, chans)
    for a in range(3):
        for b in range(3):
            wgrad_ref[9 * a + 3 * b:9 * a + 3 * b + 3] = whole[9 * b + 3 * a:9 * b + 3 * a + 3]

    for cp in sends:
        cp.wait_send()

    @pl.when(t > 0)
    def _():
        to_prev().wait_send()


def local(conv_input, saved, cotangent, gain, w_conv, w_qkv, w_out):
    chans = saved.shape[-1]
    frames, columns = saved.shape[1], saved.shape[2] * saved.shape[3]
    n_t, n_h, n_b = (lax.axis_size(x) for x in ("tm", "height", "batch"))
    tile = frames * columns
    dblk = chans // n_h
    ht = -(-27 // n_b)
    taps = n_b * ht
    sizes = (n_t, n_h, n_b, frames, columns, chans, ht)
    vmem = pl.BlockSpec(memory_space=pltpu.VMEM)
    hbm = pl.BlockSpec(memory_space=pl.ANY)
    dma = pltpu.SemaphoreType.DMA
    igrad, wgrad = pl.pallas_call(
        functools.partial(body, sizes),
        out_shape=(
            jax.ShapeDtypeStruct((tile, chans), BF16),
            jax.ShapeDtypeStruct((27, dblk, chans), BF16),
        ),
        in_specs=[vmem] * 4 + [hbm] * 3,
        out_specs=(vmem, vmem),
        scratch_shapes=[
            pltpu.VMEM((chans, 3 * chans), BF16),
            pltpu.VMEM((chans, chans), BF16),
            pltpu.VMEM((27, chans, chans), BF16),
            pltpu.VMEM((2, n_h, tile, chans), BF16),
            pltpu.VMEM((n_h, dblk, tile), BF16),
            pltpu.VMEM((n_t, n_h, dblk, tile), BF16),
            pltpu.VMEM((n_h + 2, tile, chans), BF16),
            pltpu.VMEM((n_t, n_h, tile, chans), BF16),
            pltpu.VMEM((n_t, 9, n_h + 2, dblk, tile), BF16),
            pltpu.VMEM((9, tile, chans), BF16),
            pltpu.VMEM((taps, dblk, chans), F32),
            pltpu.VMEM((taps, dblk, chans), BF16),
            pltpu.VMEM((n_b, ht, dblk, chans), BF16),
            pltpu.VMEM((n_b, ht, dblk, chans), BF16),
            pltpu.VMEM((tile, chans), BF16),
            pltpu.VMEM((tile, chans), BF16),
            dma((3,)), dma((2 * frames, n_h)), dma((2 * frames, n_h)), dma((n_t, n_h)), dma((n_t, n_h)),
            dma((frames * n_t, n_h)), dma((frames * n_t, n_h)), dma, dma,
            dma((n_b,)), dma((n_b,)), dma((n_b,)), dma((n_b,)),
        ],
        compiler_params=pltpu.CompilerParams(
            collective_id=0, has_side_effects=True, vmem_limit_bytes=56 * 1024 * 1024
        ),
    )(
        saved.reshape(tile, chans), cotangent.reshape(tile, chans), conv_input.reshape(tile, chans),
        gain.reshape(1, chans), w_qkv, w_out, w_conv.reshape(27, chans, chans),
    )
    weight_grad = wgrad.astype(F32).transpose(1, 0, 2)
    return igrad.reshape(conv_input.shape), weight_grad


def solution(mesh):
    banded = P("batch", "tm", "height", None, None)
    return jax.shard_map(
        local,
        mesh=mesh,
        in_specs=(banded, banded, banded, P(), P(), P(), P()),
        out_specs=(banded, P("height", None, None)),
        check_vma=False,
    )
```

```python
import functools
import math

import jax
import jax.numpy as jnp
from jax import lax
from jax.experimental import pallas as pl
from jax.experimental.pallas import tpu as pltpu
from jax.sharding import PartitionSpec as P

EPS = 1e-06
NT = (((1,), (1,)), ((), ()))
TN = (((0,), (0,)), ((), ()))
F32 = jnp.float32
BF16 = jnp.bfloat16


def mm(x, y):
    return jnp.dot(x, y, preferred_element_type=F32)


def mm_nt(x, y):
    return lax.dot_general(x, y, NT, preferred_element_type=F32)


def mm_tn(x, y):
    return lax.dot_general(x, y, TN, preferred_element_type=F32)


def body(
    sizes,
    saved_ref, cot_ref, conv_ref, gain_ref, wqkv_hbm, wout_hbm, wconv_hbm,
    igrad_ref, wgrad_ref,
    wqkv, wout, wconv, xall, conv_t, recv_t, gpad, gall, lhs, win,
    part_f, part_b, got1, total, ig_send, ig_got,
    wsem, gs_sem, gr_sem, cs_sem, cr_sem, xs_sem, xr_sem, is_sem, ir_sem,
    s1s, s1r, s4s, s4r,
):
    n_t, n_h, n_b, frames, columns, chans, ht = sizes
    tile = frames * columns
    dblk = chans // n_h
    n_a = n_h // 2
    t = lax.axis_index("tm")
    h = lax.axis_index("height")
    c = lax.axis_index("batch")
    scale = 1.0 / math.sqrt(chans)
    norm = 1.0 / math.sqrt(n_b * n_t * frames * n_h * columns)

    loads = [
        pltpu.make_async_copy(wqkv_hbm, wqkv, wsem.at[0]),
        pltpu.make_async_copy(wout_hbm, wout, wsem.at[1]),
        pltpu.make_async_copy(wconv_hbm, wconv, wsem.at[2]),
    ]
    for load in loads:
        load.start()

    def remote(src, dst, ssem, rsem, dev):
        return pltpu.make_async_remote_copy(
            src_ref=src, dst_ref=dst, send_sem=ssem, recv_sem=rsem,
            device_id=dev, device_id_type=pl.DeviceIdType.MESH,
        )

    barrier = pltpu.get_barrier_semaphore()
    for dt in range(n_t):
        for dh in range(n_h):
            if dt or dh:
                pl.semaphore_signal(
                    barrier, inc=1,
                    device_id=(lax.rem(t + dt, n_t), lax.rem(h + dh, n_h), c),
                    device_id_type=pl.DeviceIdType.MESH,
                )
    for db in range(1, n_b):
        pl.semaphore_signal(
            barrier, inc=1, device_id=(t, h, lax.rem(c + db, n_b)),
            device_id_type=pl.DeviceIdType.MESH,
        )
    pl.semaphore_wait(barrier, n_t * n_h - 1 + n_b - 1)

    h_a, h_b = h // 2, lax.rem(h, 2)
    mate = h_a * 2 + (1 - h_b)
    order = sorted(range(1, n_a), key=lambda k: min(k, n_a - k))
    sends = []
    mine = (saved_ref, cot_ref)

    def block(f, arr, src, slot, dev, own=False):
        rows = pl.ds(f * columns, columns)
        dst = xall.at[arr, src, rows]
        return remote(
            mine[arr].at[rows] if own else dst, dst,
            gs_sem.at[2 * f + arr, slot], gr_sem.at[2 * f + arr, src], (t, dev, c),
        )

    def send_own(f):
        for arr in range(2):
            cp = block(f, arr, h, 0, mate, True)
            cp.start()
            sends.append(cp)
            for k in order:
                cp = block(f, arr, h, k, lax.rem(h_a + k, n_a) * 2 + h_b, True)
                cp.start()
                sends.append(cp)

    def pass_on(f, arr, k):
        src = lax.rem(h_a + k, n_a) * 2 + h_b
        block(f, arr, src, k, mate).wait_recv()
        cp = block(f, arr, src, n_a + k - 1, mate)
        cp.start()
        sends.append(cp)

    def arrived(f, arr):
        for k in range(n_a):
            src = lax.rem(h_a + k, n_a) * 2 + (1 - h_b)
            block(f, arr, src, 0, mate).wait_recv()

    send_own(0)
    for arr in range(2):
        xall[arr, h] = mine[arr][...]

    flipped = conv_ref[...].astype(F32).T.astype(BF16)
    for k in range(n_h):
        conv_t[k] = flipped[k * dblk:(k + 1) * dblk]
    recv_t[t, h] = conv_t[h]

    for arr in range(2):
        for k in order:
            pass_on(0, arr, k)
    for f in range(1, frames):
        send_own(f)

    for m in range(n_t):
        for k in range(n_h):
            if m or k:
                dt, peer = lax.rem(t + m, n_t), lax.rem(h + k, n_h)
                cp = remote(conv_t.at[peer], recv_t.at[t, h], cs_sem.at[m, k], cr_sem.at[t, h], (dt, peer, c))
                cp.start()
                sends.append(cp)

    def across_tm(f, m, j):
        rows = pl.ds(f * columns, columns)
        src = 2 * j + h_b
        return remote(
            gpad.at[1 + src, rows], gall.at[t, src, rows],
            xs_sem.at[f * n_t + m, j], xr_sem.at[f * n_t + t, src], (lax.rem(t + m, n_t), h, c),
        )

    def to_mate(f, m, j, parity):
        rows = pl.ds(f * columns, columns)
        frm, src = lax.rem(t + m, n_t), 2 * j + parity
        return remote(
            gall.at[frm, src, rows], gall.at[frm, src, rows],
            xs_sem.at[f * n_t + m, n_a + j], xr_sem.at[f * n_t + frm, src], (t, mate, c),
        )

    def relay(f, j):
        for m in range(1, n_t):
            cp = to_mate(f, m, j, h_b)
            cp.wait_recv()
            cp.start()
            sends.append(cp)

    loads[0].wait()
    loads[1].wait()
    gain = gain_ref[...]
    keys_n = n_h * columns
    gpad[0] = jnp.zeros_like(gpad[0])
    gpad[n_h + 1] = jnp.zeros_like(gpad[0])

    for f in range(frames):
        rows = pl.ds(f * columns, columns)
        coming = [(f + 1, arr, k) for arr in range(2) for k in order] if f + 1 < frames else []
        arrived(f, 0)
        hidden = xall[0, :, rows, :].reshape(keys_n, chans).astype(F32)
        inverse = lax.rsqrt(jnp.mean(hidden * hidden, -1, keepdims=True) + EPS)
        normed = (hidden * inverse * gain).astype(BF16)
        qkv = mm(normed, wqkv[...]).astype(BF16)
        q, k, v = qkv[:, :chans], qkv[:, chans:2 * chans], qkv[:, 2 * chans:]
        s = mm_nt(k, q) * scale
        e = jnp.exp(s - jnp.max(s, 0, keepdims=True))
        p = e / jnp.sum(e, 0, keepdims=True)
        arrived(f, 1)
        for item in coming[:len(order) // 2]:
            pass_on(*item)
        cot = xall[1, :, rows, :].reshape(keys_n, chans)
        go = mm_nt(cot, wout[...]).astype(BF16)
        gp = mm_nt(v, go)
        delta = jnp.sum(p * gp, 0, keepdims=True)
        gs = (p * (gp - delta) * scale).astype(BF16)
        gq = mm_tn(gs, k).astype(BF16)
        gk = mm(gs, q).astype(BF16)
        gv = mm(p.astype(BF16), go).astype(BF16)
        for item in coming[len(order) // 2:len(order)]:
            pass_on(*item)
        gn = (
            mm_nt(gq, wqkv[:, :chans])
            + mm_nt(gk, wqkv[:, chans:2 * chans])
            + mm_nt(gv, wqkv[:, 2 * chans:])
        )
        scaled = gn * gain
        g = cot.astype(F32) + inverse * (
            scaled - hidden * inverse * inverse * jnp.mean(scaled * hidden, -1, keepdims=True)
        )
        gpad[1:n_h + 1, rows, :] = g.astype(BF16).reshape(n_h, columns, chans)
        for j in range(n_a):
            for m in range(1, n_t):
                cp = across_tm(f, m, j)
                cp.start()
                sends.append(cp)
        for item in coming[len(order):]:
            pass_on(*item)

    for m in range(n_t):
        for k in range(n_h):
            if m or k:
                frm, src = lax.rem(t + m, n_t), lax.rem(h + k, n_h)
                remote(conv_t.at[0], recv_t.at[frm, src], cs_sem.at[m, k], cr_sem.at[frm, src], (frm, src, c)).wait_recv()

    for f in range(frames - 1):
        for j in range(n_a):
            relay(f, j)

    lane = lax.broadcasted_iota(jnp.int32, (dblk, tile), 1)
    for m in range(n_t):
        for i in range(9):
            lhs[m, i, 0] = jnp.zeros((dblk, tile), BF16)
            lhs[m, i, n_h + 1] = jnp.zeros((dblk, tile), BF16)

    def build(m):
        frm = lax.rem(t + m, n_t)
        before = jnp.maximum(frm - 1, 0)

        def shifts(r, carry):
            own = recv_t[frm, r].astype(F32)
            prev = jnp.where(frm > 0, recv_t[before, r].astype(F32), 0.0)
            both = jnp.where(lane < columns, pltpu.roll(prev, columns, 1), pltpu.roll(own, columns, 1))
            for a, x in enumerate((prev, both, own)):
                left = jnp.where(lax.rem(lane, columns) == 0, 0.0, pltpu.roll(x, 1, 1))
                right = jnp.where(lax.rem(lane, columns) == columns - 1, 0.0, pltpu.roll(x, tile - 1, 1))
                for j, y in enumerate((left, x, right)):
                    lhs[m, 3 * a + j, r + 1] = y.astype(BF16)
            return carry

        lax.fori_loop(0, n_h, shifts, 0)

    def product(m, b, rights):
        left = jnp.concatenate(
            [lhs[m, :, b + r].reshape(9 * dblk, tile) for r in range(n_h)], axis=1
        )
        return mm(left, rights).reshape(9, dblk, chans)

    build(0)
    for tap in range(27, n_b * ht):
        part_f[tap] = jnp.zeros((dblk, chans), F32)
        part_b[tap] = jnp.zeros((dblk, chans), BF16)
    rights = gpad[1:n_h + 1].reshape(n_h * tile, chans)
    spots = [(j * 3) // n_a for j in range(n_a)]
    for b in range(3):
        part_f[9 * b:9 * b + 9] = product(0, b, rights)
        for j in range(n_a - 1):
            if spots[j] == b:
                relay(frames - 1, j)
    for j in range(n_a - 1):
        if spots[j] > 2:
            relay(frames - 1, j)

    row = lax.broadcasted_iota(jnp.int32, (tile, chans), 0)
    for b in range(3):
        x = gpad[h + 2 - b].astype(F32)
        ahead = jnp.where(lax.rem(row, columns) == columns - 1, 0.0, pltpu.roll(x, tile - 1, 0))
        behind = jnp.where(lax.rem(row, columns) == 0, 0.0, pltpu.roll(x, 1, 0))
        for j, y in enumerate((ahead, x, behind)):
            win[3 * b + j] = y.astype(BF16)
    loads[2].wait()

    def taps(a):
        acc = mm_nt(win[0], wconv[9 * a])
        for i in range(1, 9):
            acc = acc + mm_nt(win[i], wconv[9 * a + i])
        return acc

    y0 = taps(0)
    relay(frames - 1, n_a - 1)
    y1 = taps(1)
    cut = columns
    ig_send[...] = jnp.concatenate([y0[:cut], y0[cut:] + y1[:cut]], 0).astype(BF16)

    def to_prev():
        return remote(ig_send, ig_got, is_sem, ir_sem, (jnp.maximum(t - 1, 0), h, c))

    @pl.when(t > 0)
    def _():
        to_prev().start()

    @pl.when(t == n_t - 1)
    def _():
        ig_got[...] = jnp.zeros_like(ig_got)

    for m in range(1, n_t):
        build(m)

    halves = [
        remote(
            part_b.at[pl.ds(lax.rem(c + k, n_b) * ht, ht)], got1.at[c], s1s.at[k], s1r.at[c],
            (t, h, lax.rem(c + k, n_b)),
        )
        for k in range(1, n_b)
    ]
    sends += halves
    for m in range(1, n_t):
        for f in range(frames):
            for j in range(n_a):
                to_mate(f, m, j, 1 - h_b).wait_recv()
    for m in range(1, max(n_t, 2)):
        rights = gall[lax.rem(t + m, n_t)].reshape(n_h * tile, chans)
        for i in range(3):
            b = jnp.where(c == 0, 2 - i, i)
            out = part_f[pl.ds(9 * b, 9)]
            if n_t > 1:
                out = out + product(m, b, rights)
            if m == max(n_t, 2) - 1:
                out = out * norm
                part_b[pl.ds(9 * b, 9)] = out.astype(BF16)
            part_f[pl.ds(9 * b, 9)] = out
            if m == max(n_t, 2) - 1 and i == (1 if n_b == 2 and ht <= 18 else 2):
                for cp in halves:
                    cp.start()

    y2 = taps(2)
    own_ig = y2 + jnp.concatenate([y1[cut:], jnp.zeros((tile - cut, chans), F32)], 0)

    acc = part_f[pl.ds(c * ht, ht)]
    for k in range(1, n_b):
        peer = lax.rem(c + k, n_b)
        remote(part_b.at[pl.ds(0, ht)], got1.at[peer], s1s.at[k], s1r.at[peer], (t, h, peer)).wait_recv()
        acc = acc + got1[peer].astype(F32)
    total[c] = acc.astype(BF16)
    for k in range(1, n_b):
        cp = remote(total.at[c], total.at[c], s4s.at[k], s4r.at[c], (t, h, lax.rem(c + k, n_b)))
        cp.start()
        sends.append(cp)

    @pl.when(t < n_t - 1)
    def _():
        to_prev().wait_recv()

    igrad_ref[...] = (own_ig + ig_got[...].astype(F32)).astype(BF16)

    for k in range(1, n_b):
        peer = lax.rem(c + k, n_b)
        remote(total.at[peer], total.at[peer], s4s.at[k], s4r.at[peer], (t, h, peer)).wait_recv()
    whole = total.reshape(n_b * ht, dblk, chans)
    for a in range(3):
        for b in range(3):
            wgrad_ref[9 * a + 3 * b:9 * a + 3 * b + 3] = whole[9 * b + 3 * a:9 * b + 3 * a + 3]

    for cp in sends:
        cp.wait_send()

    @pl.when(t > 0)
    def _():
        to_prev().wait_send()


def local(conv_input, saved, cotangent, gain, w_conv, w_qkv, w_out):
    chans = saved.shape[-1]
    frames, columns = saved.shape[1], saved.shape[2] * saved.shape[3]
    n_t, n_h, n_b = (lax.axis_size(x) for x in ("tm", "height", "batch"))
    tile = frames * columns
    dblk = chans // n_h
    ht = -(-27 // n_b)
    taps = n_b * ht
    sizes = (n_t, n_h, n_b, frames, columns, chans, ht)
    vmem = pl.BlockSpec(memory_space=pltpu.VMEM)
    hbm = pl.BlockSpec(memory_space=pl.ANY)
    dma = pltpu.SemaphoreType.DMA
    igrad, wgrad = pl.pallas_call(
        functools.partial(body, sizes),
        out_shape=(
            jax.ShapeDtypeStruct((tile, chans), BF16),
            jax.ShapeDtypeStruct((27, dblk, chans), BF16),
        ),
        in_specs=[vmem] * 4 + [hbm] * 3,
        out_specs=(vmem, vmem),
        scratch_shapes=[
            pltpu.VMEM((chans, 3 * chans), BF16),
            pltpu.VMEM((chans, chans), BF16),
            pltpu.VMEM((27, chans, chans), BF16),
            pltpu.VMEM((2, n_h, tile, chans), BF16),
            pltpu.VMEM((n_h, dblk, tile), BF16),
            pltpu.VMEM((n_t, n_h, dblk, tile), BF16),
            pltpu.VMEM((n_h + 2, tile, chans), BF16),
            pltpu.VMEM((n_t, n_h, tile, chans), BF16),
            pltpu.VMEM((n_t, 9, n_h + 2, dblk, tile), BF16),
            pltpu.VMEM((9, tile, chans), BF16),
            pltpu.VMEM((taps, dblk, chans), F32),
            pltpu.VMEM((taps, dblk, chans), BF16),
            pltpu.VMEM((n_b, ht, dblk, chans), BF16),
            pltpu.VMEM((n_b, ht, dblk, chans), BF16),
            pltpu.VMEM((tile, chans), BF16),
            pltpu.VMEM((tile, chans), BF16),
            dma((3,)), dma((2 * frames, n_h)), dma((2 * frames, n_h)), dma((n_t, n_h)), dma((n_t, n_h)),
            dma((frames * n_t, n_h)), dma((frames * n_t, n_h)), dma, dma,
            dma((n_b,)), dma((n_b,)), dma((n_b,)), dma((n_b,)),
        ],
        compiler_params=pltpu.CompilerParams(
            collective_id=0, has_side_effects=True, vmem_limit_bytes=56 * 1024 * 1024
        ),
    )(
        saved.reshape(tile, chans), cotangent.reshape(tile, chans), conv_input.reshape(tile, chans),
        gain.reshape(1, chans), w_qkv, w_out, w_conv.reshape(27, chans, chans),
    )
    weight_grad = wgrad.astype(F32).transpose(1, 0, 2)
    return igrad.reshape(conv_input.shape), weight_grad


def solution(mesh):
    banded = P("batch", "tm", "height", None, None)
    return jax.shard_map(
        local,
        mesh=mesh,
        in_specs=(banded, banded, banded, P(), P(), P(), P()),
        out_specs=(banded, P("height", None, None)),
        check_vma=False,
    )
```
